32 devices in a mesh: peer: 16 (over z, y, x), tp: 2 (over core).
Axes of the slice: x: 2, y: 2, z: 4, core: 2. Of those that a mesh axis runs over, the one named last changes fastest.
Arguments:
- grad_blocks: bfloat16 [6144, 6656], P('peer', 'tp'), may hold values from -6 to 6
- row_scale: float32 [6144], P('peer'), may hold values from 0.25 to 4
- dest_peer: int32 [6144, 1], P('peer'), may hold values from 0 to 15; in each aligned block of 384 rows (0 to 383, 384 to 767, ...) at most 48 rows name the same one
- dest_slot: int32 [6144], P('peer'), may hold values from 0 to 383
- doc_ids: int32 [16, 384], P('peer'), may hold values from 0 to 23, never falling along the last dimension, each value on 1 to 192 neighbouring positions
- query_rows: bfloat16 [6144, 6144], P('peer', 'tp'), may hold values from -21 to 21
- key_rows: bfloat16 [6144, 6144], P('peer', 'tp'), may hold values from -3 to 3
- value_rows: bfloat16 [6144, 6144], P('peer', 'tp'), may hold values from -6 to 6
- out_weight: bfloat16 [6144, 6656], P('tp', 'peer'), may hold values from -0.078125 to 0.078125
Outputs:
- grad_q: bfloat16 [6144, 6144], P('peer', 'tp')
- grad_k: bfloat16 [6144, 6144], P('peer', 'tp')
- grad_v: bfloat16 [6144, 6144], P('peer', 'tp')
The draws below stay inside these ranges and needn't reach their ends.
Inputs may be any that keep to these rules, and one draw needn't show every extreme that they name: `dest_peer`: no peer is named by more than 48 rows of one device, and in every draw some peer is named by exactly 48 rows of some device. `doc_ids`: along each row of 384 the ids never fall; a document has at most half of 384 positions.
All inputs are finite; a program needn't handle non-finite values.
Results may differ from the reference program's by a relative error of at most 0.014.
Values may be sent and summed in bfloat16 or wider, within the bound.
No kernel may reach another device: no remote copies, remote signals or barrier semaphores. Data moves between devices by JAX's collectives and lax.ppermute only.
A program may use at most 192 MiB of HBM per device.

```python
import math
import jax
import jax.numpy as jnp
import numpy as np
from jax import lax

D = 6656
HS = 128
TOK_DEV = 384
TOKENS = 6144
PEERS = 16
HD = 6144
CAP = 48
N_PEER = 16


def draw_key_rows(key, part):
    key = jax.random.fold_in(key, 11)
    result = jax.random.truncated_normal(key, -3.0, 3.0, (TOKENS, HD), jnp.float32)
    return result.astype(jnp.bfloat16)


def draw_query_rows(key, part):
    key = jax.random.fold_in(key, 12)
    result = jax.random.truncated_normal(key, -3.0, 3.0, (TOKENS, HD), jnp.float32)
    return result.astype(jnp.bfloat16)


def plant(values, own_key, low, top_value):
    extent = values.shape
    spot = [jax.random.randint(jax.random.fold_in(own_key, axis), (), 0, extent[axis]) for axis in range(len(extent))]
    values = values.at[tuple(spot)].set(low)
    longest = extent.index(max(extent))
    spot[longest] = (spot[longest] + 1) % extent[longest]
    return values.at[tuple(spot)].set(top_value)


def block_scale(key, dims, split, low, largest):
    def one(dim, parts):
        draws = jax.random.uniform(jax.random.fold_in(jax.random.fold_in(key, 6), dim), (parts,), jnp.float32, low / len(split), largest / len(split))
        return jnp.repeat(jnp.exp(draws), dims[dim] // parts).reshape((-1,) + (1,) * (len(dims) - dim - 1))

    loudness = one(*split[0])
    for cut in split[1:]:
        loudness = loudness * one(*cut)
    return loudness


def length_profile(number_of, total, most, skew):
    loads = [(1 << 20) // math.isqrt(standing ** skew) + 1 for standing in range(2, number_of + 1)]
    spare, counts = total - most - (number_of - 1), [1] * (number_of - 1)
    while spare > 0:
        free = [i for i in range(number_of - 1) if counts[i] < most]
        whole, left = sum([loads[i] for i in free]), spare
        for i in free:
            more = min(most - counts[i], max(1, left * loads[i] // whole), spare)
            counts[i] = counts[i] + more
            spare = spare - more
    return np.array([most] + counts)


def ragged_sizes(own_key, count, total, bound, lean):
    if count == 2:
        one = jax.random.randint(own_key, (), max(1, total - bound), min(bound, total - 1) + 1)
        return jnp.stack([one, total - one])
    sizes = jnp.asarray(length_profile(count, total, bound, lean), jnp.int32)
    twos = (count - 1) // 2
    giver, taker = sizes[1:1 + 2 * twos:2], sizes[2:2 + 2 * twos:2]
    margin = jnp.minimum(giver - 1, bound - taker)
    passed = jax.random.randint(jax.random.fold_in(own_key, 1), (twos,), 0, 1 << 20) % (margin + 1)
    sizes = sizes.at[1:1 + 2 * twos:2].set(giver - passed).at[2:2 + 2 * twos:2].set(taker + passed)
    return sizes[jax.random.permutation(jax.random.fold_in(own_key, 2), count)]


def assign_block(rng, own, number, rows, count, top, reach, lean):
    order = jax.random.permutation(rng, count)
    heavy_load, ordinary = load_shares(count, rows * top, reach, lean, True), load_shares(count, rows * top, reach, lean, False)
    places = jnp.arange(count)

    def named(tallies, rotation):
        used = int((tallies > 0).sum())
        fixed = max(1, used // 4)
        shifted = fixed + (places - fixed + rotation * (used - fixed)) % max(1, count - fixed)
        return jnp.zeros((count,), jnp.int32).at[order[jnp.where(places < fixed, places, shifted)]].set(jnp.asarray(tallies, jnp.int32))

    tallies = jnp.where(number % 4 == 0, named(heavy_load, number // 4), named(ordinary, number - number // 4 - 1))
    mixed = jax.random.permutation(jax.random.fold_in(own, 3), count)
    donor, taker = mixed[0:count // 2 * 2:2], mixed[1:count // 2 * 2:2]
    room = jnp.minimum(tallies[donor] - 1, reach - tallies[taker]) // 2
    room = jnp.where((donor == order[0]) | (taker == order[0]) | (tallies[taker] == 0), 0, jnp.maximum(room, 0))
    shifted = jax.random.randint(jax.random.fold_in(own, 4), (count // 2,), 0, 1 << 20) % (room + 1)
    tallies = tallies.at[donor].add(-shifted).at[taker].add(shifted)
    members = jnp.searchsorted(jnp.cumsum(tallies), jnp.arange(rows * top), side="right").astype(jnp.int32)
    listing = members.reshape(top, rows).T
    listing = listing[jax.random.permutation(jax.random.fold_in(own, 1), rows)]
    rotation = jax.random.randint(jax.random.fold_in(own, 2), (rows, 1), 0, top)
    return jnp.take_along_axis(listing, (jnp.arange(top)[None, :] + rotation) % top, axis=1)


def load_shares(amount, total, bound, skew, full):
    loads = [(1 << 20) // math.isqrt(standing ** skew) + 1 for standing in range(1, amount + 1)]
    largest = bound if full else min(bound, max(-(-total // amount), total * loads[0] // sum(loads)))
    least = 1 if total - largest >= amount - 1 else 0
    given, surplus = [largest] + [least] * (amount - 1), total - largest - least * (amount - 1)
    while surplus > 0:
        free = [i for i in range(1, amount) if given[i] < largest] or [i for i in range(1, amount) if given[i] < bound]
        whole, remaining = sum([loads[i] for i in free]), surplus
        for i in free:
            addition = min(bound - given[i], max(1, remaining * loads[i] // whole), surplus)
            given[i] = given[i] + addition
            surplus = surplus - addition
    return np.array(given)


def noise(key, shape, deviation, reach, pieces=(), kind=jnp.bfloat16):
    values = deviation * jax.random.normal(key, shape, jnp.float32)
    if pieces:
        values = values * block_scale(key, shape, pieces, -0.22, 0.18)
    return jnp.clip(values, -reach, reach).astype(kind)


def setup_inputs(seed: int = 0) -> dict:
    arg_keys = jax.random.split(jax.random.key(seed), 10)
    grad_blocks = noise(arg_keys[0], (TOKENS, D), 1.0, 6.0, ((0, 16), (1, 2)))
    row_scale = jnp.clip(jnp.exp(math.log(4.0) - 2.7725887 * jax.random.uniform(arg_keys[1], (TOKENS,), jnp.float32) ** block_scale(arg_keys[1], (TOKENS,), ((0, 16),), -0.2, 0.2)), 0.25, 4.0)
    dest_peer_keys = jax.random.split(jax.random.fold_in(arg_keys[2], 1), TOKENS // TOK_DEV)
    dest_peer_turns = jax.random.permutation(jax.random.fold_in(arg_keys[2], 3), TOKENS // TOK_DEV)
    dest_peer = jax.vmap(lambda own, number: assign_block(jax.random.fold_in(arg_keys[2], 2), own, number, TOK_DEV, N_PEER, 1, CAP, 2))(dest_peer_keys, dest_peer_turns).reshape((TOKENS, 1))
    dest_slot = plant(jax.random.randint(arg_keys[3], (TOKENS,), 0, TOK_DEV), jax.random.fold_in(arg_keys[3], 1), 0, TOK_DEV - 1).astype(jnp.int32)
    doc_ids = jax.vmap(lambda own: jnp.searchsorted(jnp.cumsum(ragged_sizes(own, max(4, TOK_DEV // 16), TOK_DEV, TOK_DEV // 2, 2)), jnp.arange(TOK_DEV), side="right"))(jax.random.split(arg_keys[4], PEERS)).reshape((PEERS, TOK_DEV)).astype(jnp.int32)
    query_rows = draw_query_rows(jax.random.fold_in(arg_keys[9], 71), 0)
    key_rows = draw_key_rows(jax.random.fold_in(arg_keys[9], 71), 0)
    value_rows = noise(arg_keys[7], (TOKENS, HD), 1.0, 6.0, ((0, 16), (1, 2)))
    out_weight = noise(arg_keys[8], (HD, D), HD ** -0.5, 0.078125, ((0, 2), (1, 16)))
    return dict(grad_blocks=grad_blocks, row_scale=row_scale, dest_peer=dest_peer, dest_slot=dest_slot, doc_ids=doc_ids, query_rows=query_rows, key_rows=key_rows, value_rows=value_rows, out_weight=out_weight)


def attend_block(query_part, key_part, value_part, grad_part, doc_part, head_size):
    count = query_part.shape[0]

    def heads(array):
        return array.astype(jnp.float32).reshape(count, -1, head_size)
    q_heads = heads(query_part)
    k_heads = heads(key_part)
    v_heads = heads(value_part)
    g_heads = heads(grad_part)
    factor = 1.0 / math.sqrt(head_size)
    scores = jnp.einsum('ihd,jhd->hij', q_heads, k_heads) * factor
    places = jnp.arange(count, dtype=jnp.int32)
    allowed = (doc_part[:, None] == doc_part[None, :]) & (places[None, :] <= places[:, None])
    scores = jnp.where(allowed[None], scores, -1e+30)
    highest = lax.optimization_barrier(jnp.max(scores, axis=-1, keepdims=True))
    raised = jnp.exp(scores - highest)
    probs = raised / lax.optimization_barrier(jnp.sum(raised, axis=-1, keepdims=True))
    output = jnp.einsum('hij,jhd->ihd', probs, v_heads)
    delta = lax.optimization_barrier(jnp.sum(g_heads * output, axis=-1))
    probs_low = lax.optimization_barrier(probs.astype(jnp.bfloat16)).astype(jnp.float32)
    grad_v = jnp.einsum('hij,ihd->jhd', probs_low, g_heads)
    grad_p = jnp.einsum('ihd,jhd->hij', g_heads, v_heads)
    grad_s = probs * (grad_p - jnp.transpose(delta)[:, :, None])
    grad_low = lax.optimization_barrier(grad_s.astype(jnp.bfloat16)).astype(jnp.float32)
    grad_q = jnp.einsum('hij,jhd->ihd', grad_low, k_heads) * factor
    grad_k = jnp.einsum('hij,ihd->jhd', grad_low, q_heads) * factor
    return (grad_q.reshape(count, -1).astype(jnp.bfloat16), grad_k.reshape(count, -1).astype(jnp.bfloat16), grad_v.reshape(count, -1).astype(jnp.bfloat16))

def reference(grad_blocks, row_scale, dest_peer, dest_slot, doc_ids, query_rows, key_rows, value_rows, out_weight):
    target = (dest_peer[:, 0] * TOK_DEV + dest_slot).astype(jnp.int32)
    terms = row_scale[:, None] * grad_blocks.astype(jnp.float32)
    grad_out = jnp.zeros((TOKENS, D), jnp.float32).at[target].add(terms)
    grad_rows = grad_out.astype(jnp.bfloat16)
    grad_attn = jnp.dot(grad_rows, jnp.transpose(out_weight), preferred_element_type=jnp.float32).astype(jnp.bfloat16)

    def blocked(array):
        return array.reshape(PEERS, TOK_DEV, array.shape[-1])

    def one_block(packed):
        return attend_block(packed[0], packed[1], packed[2], packed[3], packed[4], HS)
    grad_q, grad_k, grad_v = lax.map(one_block, (blocked(query_rows), blocked(key_rows), blocked(value_rows), blocked(grad_attn), doc_ids))
    return (grad_q.reshape(TOKENS, HD), grad_k.reshape(TOKENS, HD), grad_v.reshape(TOKENS, HD))
```

```python
import functools
import math

import jax
import jax.numpy as jnp
from jax import lax
from jax.experimental import pallas as pl
from jax.experimental.pallas import tpu as pltpu
from jax.sharding import PartitionSpec as P

HS = 128
INNER = 4
AXES = ("peer", "tp")
PARAMS = pltpu.CompilerParams(vmem_limit_bytes=56 * 1024 * 1024)


def swap(array, peers, cores, move):
    pairs = []
    for peer in range(peers):
        for core in range(cores):
            to_peer, to_core = move(peer, core)
            pairs.append((peer * cores + core, to_peer * cores + to_core))
    return lax.ppermute(array, AXES, pairs)


def after(array, *others):
    return lax.optimization_barrier((array,) + others)[0]


def pack_kernel(position_ref, rows_ref, *out_refs):
    count = out_refs[0].shape[0]
    rows = rows_ref[...]
    for k, out_ref in enumerate(out_refs):
        places = lax.broadcasted_iota(jnp.int32, (count, rows.shape[0]), 0) + k * count
        chosen = (places == position_ref[...]).astype(jnp.float32).astype(jnp.bfloat16)
        out_ref[...] = jnp.dot(chosen, rows, preferred_element_type=jnp.float32).astype(jnp.bfloat16)


def pack(position, rows, parts, count):
    width = rows.shape[1]
    return pl.pallas_call(
        pack_kernel,
        out_shape=[jax.ShapeDtypeStruct((count, width), jnp.bfloat16)] * parts,
        compiler_params=PARAMS,
        cost_estimate=pl.CostEstimate(
            flops=2 * parts * count * rows.size, bytes_accessed=2 * (rows.size + parts * count * width), transcendentals=0
        ),
    )(position[None, :], rows)


def place_kernel(slots_ref, *refs):
    out_ref = refs[-1]
    rows = jnp.concatenate([ref[0] for ref in refs[:-1]], axis=0)
    tokens = lax.broadcasted_iota(jnp.int32, (out_ref.shape[1], rows.shape[0]), 0)
    chosen = (tokens == slots_ref[0]).astype(jnp.float32).astype(jnp.bfloat16)
    out_ref[0] = jnp.dot(chosen, rows, preferred_element_type=jnp.float32).astype(jnp.bfloat16)


def place(slots, pieces, tok_count):
    groups, capacity, width = pieces[0].shape
    total = slots.shape[2]
    return pl.pallas_call(
        place_kernel,
        grid=(groups,),
        in_specs=[pl.BlockSpec((1, 1, total), lambda t: (t, 0, 0))]
        + [pl.BlockSpec((1, capacity, width), lambda t: (t, 0, 0))] * len(pieces),
        out_specs=pl.BlockSpec((1, tok_count, width), lambda t: (t, 0, 0)),
        out_shape=jax.ShapeDtypeStruct((groups, tok_count, width), jnp.bfloat16),
        compiler_params=PARAMS,
        cost_estimate=pl.CostEstimate(
            flops=2 * groups * tok_count * total * width,
            bytes_accessed=2 * groups * width * (total + tok_count),
            transcendentals=0,
        ),
    )(slots, *pieces)


def join_kernel(own_ref, *refs):
    out_ref = refs[-1]
    for k, ref in enumerate(refs[:-1]):
        out_ref[k ^ own_ref[0]] = ref[...]


def join(own, pieces):
    depth, columns = pieces[0].shape
    joined = pl.pallas_call(
        join_kernel,
        in_specs=[pl.BlockSpec(memory_space=pltpu.SMEM)]
        + [pl.BlockSpec((depth, columns), lambda: (0, 0))] * len(pieces),
        out_shape=jax.ShapeDtypeStruct((len(pieces), depth, columns), jnp.bfloat16),
        compiler_params=PARAMS,
        cost_estimate=pl.CostEstimate(
            flops=0, bytes_accessed=4 * len(pieces) * depth * columns, transcendentals=0
        ),
    )(own.reshape(1), *pieces)
    return joined.reshape(len(pieces) * depth, columns)


def product_kernel(rows_ref, weight_ref, *refs):
    total = jnp.dot(rows_ref[0], weight_ref[...], preferred_element_type=jnp.float32)
    for ref in refs[:-1]:
        total = total + ref[0].astype(jnp.float32)
    refs[-1][0] = total.astype(jnp.bfloat16)


def product(rows, weight, block, columns, level, arrived):
    groups, tok_count, width = rows.shape
    first, step = 1 << level, 2 << level
    steps = groups // step
    in_specs = [
        pl.BlockSpec((1, tok_count, width), lambda m: (first + m * step, 0, 0)),
        pl.BlockSpec((width, columns), lambda m: (0, block)),
    ]
    for j in range(level):
        in_specs.append(
            pl.BlockSpec((1, tok_count, columns), lambda m, j=j: ((first >> (j + 1)) + m * (step >> (j + 1)), 0, 0))
        )
    return pl.pallas_call(
        product_kernel,
        grid=(steps,),
        in_specs=in_specs,
        out_specs=pl.BlockSpec((1, tok_count, columns), lambda m: (m, 0, 0)),
        out_shape=jax.ShapeDtypeStruct((steps, tok_count, columns), jnp.bfloat16),
        compiler_params=PARAMS,
        cost_estimate=pl.CostEstimate(
            flops=2 * steps * tok_count * width * columns,
            bytes_accessed=2 * (steps * tok_count * (width + columns) + width * columns),
            transcendentals=0,
        ),
    )(rows, weight, *arrived)


def attend_kernel(n_arrived, n_old, rows_ref, weight_ref, doc_ref, doc_column_ref, q_ref, k_ref, v_ref, *refs):
    arrived = refs[:n_arrived]
    dq_ref, dk_ref, dv_ref = refs[n_arrived + n_old :]
    total = jnp.dot(rows_ref[0], weight_ref[...], preferred_element_type=jnp.float32)
    for ref in arrived:
        total = total + ref[0].astype(jnp.float32)
    grad = total.astype(jnp.bfloat16)
    q, k, v = q_ref[...], k_ref[...], v_ref[...]
    count = q.shape[0]
    factor = 1.0 / math.sqrt(HS)
    across = (((1,), (1,)), ((), ()))
    down = (((0,), (0,)), ((), ()))
    scores = lax.dot_general(k, q, across, preferred_element_type=jnp.float32) * factor
    key_at = lax.broadcasted_iota(jnp.int32, (count, count), 0)
    query_at = lax.broadcasted_iota(jnp.int32, (count, count), 1)
    allowed = (doc_column_ref[...] == doc_ref[...]) & (key_at <= query_at)
    scores = jnp.where(allowed, scores, -1e30)
    raised = jnp.exp(scores - jnp.max(scores, axis=0, keepdims=True))
    probs = raised * (1.0 / jnp.sum(raised, axis=0, keepdims=True))
    grad_p = lax.dot_general(v, grad, across, preferred_element_type=jnp.float32)
    delta = jnp.sum(probs * grad_p, axis=0, keepdims=True)
    grad_s = (probs * (grad_p - delta)).astype(jnp.bfloat16)
    probs_low = probs.astype(jnp.bfloat16)
    dv_ref[...] = jnp.dot(probs_low, grad, preferred_element_type=jnp.float32).astype(jnp.bfloat16)
    dk = jnp.dot(grad_s, q, preferred_element_type=jnp.float32) * factor
    dk_ref[...] = dk.astype(jnp.bfloat16)
    dq = lax.dot_general(grad_s, k, down, preferred_element_type=jnp.float32) * factor
    dq_ref[...] = dq.astype(jnp.bfloat16)


def attend(rows, weight, first_block, first_head, heads, arrived, doc, query, key, value, old):
    tok_count, features = query.shape
    width = rows.shape[2]
    head_spec = pl.BlockSpec((tok_count, HS), lambda h: (0, first_head + h))
    in_specs = [
        pl.BlockSpec((1, tok_count, width), lambda h: (0, 0, 0)),
        pl.BlockSpec((width, HS), lambda h: (0, first_block + h)),
        pl.BlockSpec((1, tok_count), lambda h: (0, 0)),
        pl.BlockSpec((tok_count, 1), lambda h: (0, 0)),
        head_spec,
        head_spec,
        head_spec,
    ]
    in_specs += [pl.BlockSpec((1, tok_count, HS), lambda h: (0, 0, h))] * len(arrived)
    in_specs += [pl.BlockSpec(memory_space=pl.ANY)] * len(old)
    base = 7 + len(arrived)
    return pl.pallas_call(
        functools.partial(attend_kernel, len(arrived), len(old)),
        grid=(heads,),
        in_specs=in_specs,
        out_specs=[head_spec] * 3,
        out_shape=[jax.ShapeDtypeStruct((tok_count, features), jnp.bfloat16)] * 3,
        input_output_aliases={base + n: n for n in range(len(old))},
        compiler_params=PARAMS,
        cost_estimate=pl.CostEstimate(
            flops=2 * heads * tok_count * HS * (width + 5 * tok_count),
            bytes_accessed=2 * heads * HS * (width + 8 * tok_count) + 2 * tok_count * width,
            transcendentals=heads * tok_count * tok_count,
        ),
    )(rows, weight, doc, doc.reshape(tok_count, 1), query, key, value, *arrived, *old)


def shards(
    grad_blocks,
    row_scale,
    dest_peer,
    dest_slot,
    doc_ids,
    query_rows,
    key_rows,
    value_rows,
    out_weight,
):
    tok_count, width_part = grad_blocks.shape
    peers, cores = lax.axis_size("peer"), lax.axis_size("tp")
    planes = peers // INNER
    span = planes // cores
    width = width_part // span
    capacity = 2 * tok_count // peers
    room = -(-capacity // 16) * 16
    levels = planes.bit_length() - 1
    me, core = lax.axis_index("peer"), lax.axis_index("tp")
    plane, inner = me // INNER, me % INNER
    send = functools.partial(swap, peers=peers, cores=cores)

    known = (dest_peer[:, 0] * tok_count + dest_slot)[None, :]
    step = 1
    while step < peers:
        known = jnp.concatenate([known, send(known, move=lambda p, c: (p ^ step, c))], axis=0)
        step *= 2

    plane_rows = []
    for r in range(span):
        start = ((plane % span) ^ r) * width
        part = lax.dynamic_slice(grad_blocks, (0, start), (tok_count, width))
        part = (row_scale[:, None] * part.astype(jnp.float32)).astype(jnp.bfloat16)

        def move(p, c, r=r):
            o, i = p // INNER, p % INNER
            return (c * span + ((o % span) ^ r)) * INNER + i, o // span

        plane_rows.append(send(part, move=move))

    weight = out_weight.T
    n_heads = weight.shape[1] // HS
    chunk = n_heads // 6
    n_groups, per_group = 3, 2
    group_columns = chunk * per_group * HS

    def gather_weight(g, *hold):
        part = weight[:, g * group_columns : (g + 1) * group_columns]
        if hold:
            part = after(part, *hold)
        pieces = [part] + [send(part, move=lambda p, c, k=k: (p ^ k, c)) for k in range(1, INNER)]
        return join(inner, pieces)

    weights = [gather_weight(0)]

    offset = core ^ (plane // span)
    known = known.reshape(cores, span, INNER, tok_count)[offset ^ jnp.arange(cores, dtype=jnp.int32)]
    known = known.reshape(peers, tok_count)
    target, slot = known // tok_count, known % tok_count
    rows_at = jnp.arange(tok_count, dtype=jnp.int32)
    same = (target[:, :, None] == target[:, None, :]) & (rows_at[None, None, :] < rows_at[None, :, None])
    within = jnp.sum(same.astype(jnp.int32), axis=2)
    groups = ((plane ^ jnp.arange(planes, dtype=jnp.int32)) * INNER + inner)[:, None, None, None]
    here = (target[None, :, None, :] == groups) & (
        within[None, :, None, :] == jnp.arange(room, dtype=jnp.int32)[None, None, :, None]
    )
    slots = jnp.max(jnp.where(here, slot[None, :, None, :], -1), axis=3).reshape(planes, 1, peers * room)
    position = (((target % INNER) ^ inner) * planes + ((target // INNER) ^ plane)) * room + within

    pieces = [[[None] * INNER for _ in range(span)] for _ in range(cores)]
    for r in range(span):
        packed = pack(position[r * INNER], plane_rows[r], INNER, planes * room)
        for k in range(INNER):
            piece = packed[k] if k == 0 else send(packed[k], move=lambda p, c: (p ^ k, c))
            held = [piece]
            step = 1
            while step < cores:
                held = held + [send(one, move=lambda p, c: (p, c ^ step)) for one in held]
                step *= 2
            for n, one in enumerate(held):
                pieces[n][r][k] = one.reshape(planes, room, width)
    rows = place(slots, [one for by_core in pieces for by_plane in by_core for one in by_plane], tok_count)

    for g in range(1, n_groups):
        weights.append(gather_weight(g, pieces[0][span - 1][INNER - 1]))

    old, first = [], []
    for n in range(n_groups * per_group):
        group, block = n // per_group, n % per_group
        arrived = []
        for level in range(levels):
            part = product(rows, weights[group], block, chunk * HS, level, arrived)
            if level == 0 and n >= 2:
                part = after(part, first[n - 2])
            arrived.append(send(part, move=lambda p, c: (p ^ (INNER << level), c)))
        first.append(arrived[0])
        old = attend(
            rows, weights[group], block * chunk, n * chunk, chunk, arrived,
            doc_ids, query_rows, key_rows, value_rows, old,
        )
    return tuple(old)


def solution(mesh):
    return jax.shard_map(
        shards,
        mesh=mesh,
        in_specs=(
            P("peer", "tp"),
            P("peer"),
            P("peer", None),
            P("peer"),
            P("peer", None),
            P("peer", "tp"),
            P("peer", "tp"),
            P("peer", "tp"),
            P("tp", "peer"),
        ),
        out_specs=(P("peer", "tp"), P("peer", "tp"), P("peer", "tp")),
        check_vma=False,
    )
```

```python
import functools
import math

import jax
import jax.numpy as jnp
from jax import lax
from jax.experimental import pallas as pl
from jax.experimental.pallas import tpu as pltpu
from jax.sharding import PartitionSpec as P

HS = 128
INNER = 4
AXES = ("peer", "tp")
ROW_PARTS = 3
COST = pl.CostEstimate(flops=1000, bytes_accessed=1000, transcendentals=0)
PARAMS = pltpu.CompilerParams(vmem_limit_bytes=56 * 1024 * 1024)


def swap(array, peers, cores, move):
    pairs = []
    for peer in range(peers):
        for core in range(cores):
            to_peer, to_core = move(peer, core)
            pairs.append((peer * cores + core, to_peer * cores + to_core))
    return lax.ppermute(array, AXES, pairs)


def after(array, *others):
    return lax.optimization_barrier((array,) + others)[0]


def route_kernel(shift, own_ref, known_ref, position_ref, slots_ref):
    plane, inner, peers = own_ref[0], own_ref[1], slots_ref.shape[1] * INNER
    tok_count = known_ref.shape[1]
    sources, planes, room = slots_ref.shape
    span = position_ref.shape[0]
    rows = [known_ref[n : n + 1, :].astype(jnp.int32) for n in range(sources)]
    peer_at = lax.broadcasted_iota(jnp.int32, (peers, tok_count), 0)
    named = [(peer_at == (row >> shift)).astype(jnp.float32) for row in rows]
    before = (
        lax.broadcasted_iota(jnp.int32, (tok_count, tok_count), 0)
        < lax.broadcasted_iota(jnp.int32, (tok_count, tok_count), 1)
    ).astype(jnp.float32)
    counts = jnp.dot(
        jnp.concatenate(named, axis=0).astype(jnp.bfloat16),
        before.astype(jnp.bfloat16),
        preferred_element_type=jnp.float32,
    )
    group_at = lax.broadcasted_iota(jnp.int32, (max(planes, 8), tok_count), 0)
    room_at = lax.broadcasted_iota(jnp.int32, (room, tok_count), 0)
    for n, row in enumerate(rows):
        target, slot = row >> shift, (row & ((1 << shift) - 1)) + 1
        within = jnp.sum(named[n] * counts[n * peers : (n + 1) * peers], axis=0, keepdims=True).astype(jnp.int32)
        group, place_in = (target // INNER) ^ plane, (target % INNER) ^ inner
        if n < span:
            position_ref[n : n + 1, :] = (place_in * planes + group) * room + within
        here = (group_at == group) & (place_in == 0)
        high = jnp.where(here, (slot >> 4).astype(jnp.float32), 0.0)
        low = jnp.where(here, (slot & 15).astype(jnp.float32), 0.0)
        both = jnp.concatenate([high, low], axis=0).astype(jnp.bfloat16)
        filled = (room_at == within).astype(jnp.float32).astype(jnp.bfloat16)
        found = lax.dot_general(both, filled, (((1,), (1,)), ((), ())), preferred_element_type=jnp.float32)
        half = group_at.shape[0]
        value = found[:half] * 16.0 + found[half:] - 1.0
        slots_ref[n] = value[:planes].astype(jnp.int32)


def route(own, known, shift, planes, span, room):
    sources, tok_count = known.shape
    position, slots = pl.pallas_call(
        functools.partial(route_kernel, shift),
        in_specs=[pl.BlockSpec(memory_space=pltpu.SMEM), pl.BlockSpec((sources, tok_count), lambda: (0, 0))],
        out_shape=[
            jax.ShapeDtypeStruct((span, tok_count), jnp.int32),
            jax.ShapeDtypeStruct((sources, planes, room), jnp.int32),
        ],
        compiler_params=PARAMS,
        cost_estimate=COST,
    )(own, known)
    return position, jnp.transpose(slots, (1, 0, 2)).reshape(planes, 1, sources * room)


def pack_kernel(sources, position_ref, scale_ref, *refs):
    rows_refs, out_refs = refs[:sources], refs[sources:]
    count = out_refs[0].shape[1]
    for r, rows_ref in enumerate(rows_refs):
        rows = rows_ref[...]
        for k, out_ref in enumerate(out_refs):
            places = lax.broadcasted_iota(jnp.int32, (count, rows.shape[0]), 0) + k * count
            chosen = (places == position_ref[r : r + 1, :]).astype(jnp.float32)
            scale = jnp.sum(chosen * scale_ref[r : r + 1, :], axis=1, keepdims=True)
            picked = jnp.dot(chosen.astype(jnp.bfloat16), rows, preferred_element_type=jnp.float32)
            out_ref[r] = (picked * scale).astype(jnp.bfloat16)


def pack(position, scale, rows, count):
    sources, width = len(rows), rows[0].shape[1]
    return pl.pallas_call(
        functools.partial(pack_kernel, sources),
        out_shape=[jax.ShapeDtypeStruct((sources, count, width), jnp.bfloat16)] * INNER,
        compiler_params=PARAMS,
        cost_estimate=COST,
    )(position, scale, *rows)


def place_kernel(slots_ref, *refs):
    out_ref = refs[-1]
    rows = jnp.concatenate([ref[r, 0] for ref in refs[:-1] for r in range(ref.shape[0])], axis=0)
    tokens = lax.broadcasted_iota(jnp.int32, (out_ref.shape[1], rows.shape[0]), 0)
    chosen = (tokens == slots_ref[0]).astype(jnp.float32).astype(jnp.bfloat16)
    out_ref[0] = jnp.dot(chosen, rows, preferred_element_type=jnp.float32).astype(jnp.bfloat16)


def place(slots, pieces, tok_count):
    sources, groups, room, width = pieces[0].shape
    total = slots.shape[2]
    return pl.pallas_call(
        place_kernel,
        grid=(groups,),
        in_specs=[pl.BlockSpec((1, 1, total), lambda t: (t, 0, 0))]
        + [pl.BlockSpec((sources, 1, room, width), lambda t: (0, t, 0, 0))] * len(pieces),
        out_specs=pl.BlockSpec((1, tok_count, width), lambda t: (t, 0, 0)),
        out_shape=jax.ShapeDtypeStruct((groups, tok_count, width), jnp.bfloat16),
        compiler_params=PARAMS,
        cost_estimate=COST,
    )(slots, *pieces)


def product_kernel(n_rows, n_pieces, own_ref, *refs):
    leave_ref, keep_ref, weight_ref = refs[-3:]
    m, half = pl.program_id(0), pl.num_programs(0) // 2

    @pl.when(m == 0)
    def _():
        for k, ref in enumerate(refs[n_rows : n_rows + n_pieces]):
            depth = ref.shape[0]
            if n_pieces == 1:
                weight_ref[...] = ref[...]
            else:
                at = pl.multiple_of((k ^ own_ref[1]) * depth, 16)
                weight_ref[pl.ds(at, depth), :] = ref[...]

    total, start = None, 0
    for ref in refs[:n_rows]:
        stop = start + ref.shape[2]
        term = jnp.dot(ref[0], weight_ref[start:stop, :], preferred_element_type=jnp.float32)
        total = term if total is None else total + term
        start = stop

    @pl.when(m < half)
    def _():
        leave_ref[0] = total.astype(jnp.bfloat16)

    @pl.when(m >= half)
    def _():
        keep_ref[0] = total


def product(own, rows, pieces, block, columns):
    groups, tok_count = rows[0].shape[:2]
    width, half = sum(part.shape[2] for part in rows), groups // 2
    depth = pieces[0].shape[0]
    if depth % 16:
        places = jnp.arange(len(pieces), dtype=jnp.int32) ^ own[1]
        pieces = [jnp.stack(pieces)[places].reshape(width, -1)]
        depth = width
    in_specs = [pl.BlockSpec(memory_space=pltpu.SMEM)]
    in_specs += [
        pl.BlockSpec((1, tok_count, part.shape[2]), lambda m: (jnp.where(m < half, 2 * m + 1, 2 * (m - half)), 0, 0))
        for part in rows
    ]
    in_specs += [pl.BlockSpec((depth, columns), lambda m: (0, block))] * len(pieces)
    out_block = (1, tok_count, columns)
    return pl.pallas_call(
        functools.partial(product_kernel, len(rows), len(pieces)),
        grid=(groups,),
        in_specs=in_specs,
        out_specs=[
            pl.BlockSpec(out_block, lambda m: (jnp.minimum(m, half - 1), 0, 0)),
            pl.BlockSpec(out_block, lambda m: (jnp.maximum(m - half, 0), 0, 0)),
        ],
        out_shape=[
            jax.ShapeDtypeStruct((half, tok_count, columns), jnp.bfloat16),
            jax.ShapeDtypeStruct((half, tok_count, columns), jnp.float32),
        ],
        scratch_shapes=[pltpu.VMEM((width, columns), jnp.bfloat16)],
        compiler_params=PARAMS,
        cost_estimate=COST,
    )(own, *rows, *pieces)


def attend_kernel(heads, n_parts, *refs):
    parts = refs[:n_parts]
    doc_ref, doc_column_ref, q_ref, k_ref, v_ref = refs[n_parts : n_parts + 5]
    dq_ref, dk_ref, dv_ref = refs[-3:]
    count = q_ref.shape[0]
    factor = 1.0 / math.sqrt(HS)
    across = (((1,), (1,)), ((), ()))
    down = (((0,), (0,)), ((), ()))
    key_at = lax.broadcasted_iota(jnp.int32, (count, count), 0)
    query_at = lax.broadcasted_iota(jnp.int32, (count, count), 1)
    allowed = (doc_column_ref[...] == doc_ref[...]) & (key_at <= query_at)
    for h in range(heads):
        at = slice(h * HS, (h + 1) * HS)
        total = parts[0][0, :, at]
        for ref in parts[1:]:
            total = total + ref[0, :, at].astype(jnp.float32)
        grad = total.astype(jnp.bfloat16)
        q, k, v = q_ref[:, at], k_ref[:, at], v_ref[:, at]
        scores = lax.dot_general(k, q, across, preferred_element_type=jnp.float32) * factor
        scores = jnp.where(allowed, scores, -1e30)
        raised = jnp.exp(scores - jnp.max(scores, axis=0, keepdims=True))
        probs = raised * (1.0 / jnp.sum(raised, axis=0, keepdims=True))
        grad_p = lax.dot_general(v, grad, across, preferred_element_type=jnp.float32)
        delta = jnp.sum(probs * grad_p, axis=0, keepdims=True)
        grad_s = (probs * (grad_p - delta)).astype(jnp.bfloat16)
        probs_low = probs.astype(jnp.bfloat16)
        dv_ref[:, at] = jnp.dot(probs_low, grad, preferred_element_type=jnp.float32).astype(jnp.bfloat16)
        dk = jnp.dot(grad_s, q, preferred_element_type=jnp.float32) * factor
        dk_ref[:, at] = dk.astype(jnp.bfloat16)
        dq = lax.dot_general(grad_s, k, down, preferred_element_type=jnp.float32) * factor
        dq_ref[:, at] = dq.astype(jnp.bfloat16)


def attend(parts, first_head, heads, doc, query, key, value, old):
    tok_count, features = query.shape
    columns = heads * HS
    block = first_head // heads
    chunk_spec = pl.BlockSpec((tok_count, columns), lambda i: (0, block))
    in_specs = [pl.BlockSpec((1, tok_count, columns), lambda i: (0, 0, 0))] * len(parts)
    in_specs += [
        pl.BlockSpec((1, tok_count), lambda i: (0, 0)),
        pl.BlockSpec((tok_count, 1), lambda i: (0, 0)),
        chunk_spec,
        chunk_spec,
        chunk_spec,
    ]
    in_specs += [pl.BlockSpec(memory_space=pl.ANY)] * len(old)
    base = len(parts) + 5
    return pl.pallas_call(
        functools.partial(attend_kernel, heads, len(parts)),
        grid=(1,),
        in_specs=in_specs,
        out_specs=[chunk_spec] * 3,
        out_shape=[jax.ShapeDtypeStruct((tok_count, features), jnp.bfloat16)] * 3,
        input_output_aliases={base + n: n for n in range(len(old))},
        compiler_params=PARAMS,
        cost_estimate=COST,
    )(*parts, doc, doc.reshape(tok_count, 1), query, key, value, *old)


def cut(total, parts):
    tiles = total // 128
    sizes = [tiles // parts * 128 + (128 if n < tiles % parts else 0) for n in range(parts)]
    sizes[-1] += total - sum(sizes)
    return sizes


def shards(
    grad_blocks,
    row_scale,
    dest_peer,
    dest_slot,
    doc_ids,
    query_rows,
    key_rows,
    value_rows,
    out_weight,
):
    tok_count, width_part = grad_blocks.shape
    peers, cores = lax.axis_size("peer"), lax.axis_size("tp")
    planes = peers // INNER
    span = planes // cores
    width = width_part // span
    capacity = 2 * tok_count // peers
    room = -(-capacity // 16) * 16
    levels = planes.bit_length() - 1
    me, core = lax.axis_index("peer"), lax.axis_index("tp")
    plane, inner = me // INNER, me % INNER
    own = jnp.stack([plane, inner]).astype(jnp.int32)
    send = functools.partial(swap, peers=peers, cores=cores)

    def to_plane(array, r):
        def move(p, c):
            o, i = p // INNER, p % INNER
            return (c * span + ((o % span) ^ r)) * INNER + i, o // span

        return send(array, move=move)

    shift = (tok_count - 1).bit_length()
    known = ((dest_peer[:, 0] << shift) + dest_slot).astype(jnp.float32)
    known = jnp.stack([known, row_scale])
    near = jnp.stack([to_plane(known, r) for r in range(span)])
    known, scale = near[:, 0], near[:, 1]
    for step in (1, 2):
        known = jnp.concatenate([known, send(known, move=lambda p, c: (p ^ step, c))], axis=0)
    position, slots = route(own, known, shift, planes, span, room)

    widths = cut(width, ROW_PARTS)
    plane_rows, start = [], 0
    for size in widths:
        parts = []
        for r in range(span):
            at = ((plane % span) ^ r) * width + start
            part = lax.dynamic_slice(grad_blocks, (0, at), (tok_count, size))
            part = after(part, near)
            parts.append(to_plane(part, r))
        plane_rows.append(parts)
        start += size

    weight = out_weight.T
    n_heads = weight.shape[1] // HS
    sixth = n_heads // 6
    heads = [sixth] * 5 + ([sixth // 2] * 2 if sixth % 2 == 0 else [sixth])
    firsts = [sum(heads[:n]) for n in range(len(heads))]
    group_of = [0, 0, 0] + [1] * (len(heads) - 3)
    group_first = [0, 3 * sixth, n_heads]

    def gather_weight(g, hold):
        part = weight[:, group_first[g] * HS : group_first[g + 1] * HS]
        if hold is not None:
            part = after(part, hold)
        members = [[n * INNER + k for k in range(INNER)] for n in range(planes)]
        return [lax.all_gather(part, "peer", axis=0, tiled=True, axis_index_groups=members)]

    weights = [gather_weight(0, None)]

    rows, last, packed = [], None, None
    for parts in plane_rows:
        if packed is not None:
            parts = [after(parts[0], packed[0])] + parts[1:]
        packed = pack(position, scale, parts, planes * room)
        pieces = [packed[0]] + [send(packed[k], move=lambda p, c: (p ^ k, c)) for k in range(1, INNER)]
        if last is not None:
            pieces[0] = after(pieces[0], last)
        summed = place(slots, [one.reshape(span, planes, room, one.shape[2]) for one in pieces], tok_count)
        last = summed
        step = 1
        while step < cores:
            other = send(summed, move=lambda p, c: (p, c ^ step))
            summed = (summed.astype(jnp.float32) + other.astype(jnp.float32)).astype(jnp.bfloat16)
            step *= 2
        rows.append(summed)

    weights.append(gather_weight(1, last))

    count = len(heads)
    last = rows[-1]
    leaving, arrived, kept = {}, {}, {}
    old = []

    def multiply(n):
        nonlocal last
        g = group_of[n]
        pieces = weights[g]
        first = (firsts[n] - group_first[g]) // heads[n]
        leaving[n], kept[n] = product(own, rows, [after(pieces[0], last)] + pieces[1:], first, heads[n] * HS)
        last = leaving[n]

    def launch(n, level, part):
        arrived.setdefault(n, []).append(send(part, move=lambda p, c: (p ^ (INNER << level), c)))

    def pass_on(n, level, *hold):
        nonlocal last
        part = after(kept[n], last, *hold)[1 << (level - 1) :: 1 << level]
        for j, one in enumerate(arrived[n]):
            part = part + one[1 << (level - j - 1) :: 1 << (level - j)].astype(jnp.float32)
        last = part.astype(jnp.bfloat16)
        launch(n, level, last)

    def finish(n):
        nonlocal old, last
        parts = [after(kept[n], last)] + arrived[n]
        old = attend(parts, firsts[n], heads[n], doc_ids, query_rows, key_rows, value_rows, old)
        last = old[0]

    for n in range(3):
        multiply(n)
        if n < 2:
            launch(n, 0, leaving[n])
    for n in range(count):
        for level in range(1, levels):
            pass_on(n, level, *(arrived[n - 1][-1:] if n else []))
        if n + 2 < count:
            launch(n + 2, 0, after(leaving[n + 2], last))
        if n + 3 < count:
            multiply(n + 3)
        if n >= 1:
            finish(n - 1)
    finish(count - 1)
    return tuple(old)


def solution(mesh):
    return jax.shard_map(
        shards,
        mesh=mesh,
        in_specs=(
            P("peer", "tp"),
            P("peer"),
            P("peer", None),
            P("peer"),
            P("peer", None),
            P("peer", "tp"),
            P("peer", "tp"),
            P("peer", "tp"),
            P("tp", "peer"),
        ),
        out_specs=(P("peer", "tp"), P("peer", "tp"), P("peer", "tp")),
        check_vma=False,
    )
```

```python
import functools
import math

import jax
import jax.numpy as jnp
from jax import lax
from jax.experimental import pallas as pl
from jax.experimental.pallas import tpu as pltpu
from jax.sharding import PartitionSpec as P

HS = 128
INNER = 4
AXES = ("peer", "tp")
ROW_PARTS = 3
COST = pl.CostEstimate(flops=1000, bytes_accessed=1000, transcendentals=0)
PARAMS = pltpu.CompilerParams(vmem_limit_bytes=56 * 1024 * 1024)


def swap(array, peers, cores, move):
    pairs = []
    for peer in range(peers):
        for core in range(cores):
            to_peer, to_core = move(peer, core)
            pairs.append((peer * cores + core, to_peer * cores + to_core))
    return lax.ppermute(array, AXES, pairs)


def after(array, *others):
    return lax.optimization_barrier((array,) + others)[0]


def route_kernel(shift, own_ref, known_ref, position_ref, slots_ref):
    plane, inner, peers = own_ref[0], own_ref[1], slots_ref.shape[1] * INNER
    tok_count = known_ref.shape[1]
    sources, planes, room = slots_ref.shape
    span = position_ref.shape[0]
    rows = [known_ref[n : n + 1, :].astype(jnp.int32) for n in range(sources)]
    peer_at = lax.broadcasted_iota(jnp.int32, (peers, tok_count), 0)
    named = [(peer_at == (row >> shift)).astype(jnp.float32) for row in rows]
    before = (
        lax.broadcasted_iota(jnp.int32, (tok_count, tok_count), 0)
        < lax.broadcasted_iota(jnp.int32, (tok_count, tok_count), 1)
    ).astype(jnp.float32)
    counts = jnp.dot(
        jnp.concatenate(named, axis=0).astype(jnp.bfloat16),
        before.astype(jnp.bfloat16),
        preferred_element_type=jnp.float32,
    )
    group_at = lax.broadcasted_iota(jnp.int32, (max(planes, 8), tok_count), 0)
    room_at = lax.broadcasted_iota(jnp.int32, (room, tok_count), 0)
    for n, row in enumerate(rows):
        target, slot = row >> shift, (row & ((1 << shift) - 1)) + 1
        within = jnp.sum(named[n] * counts[n * peers : (n + 1) * peers], axis=0, keepdims=True).astype(jnp.int32)
        group, place_in = (target // INNER) ^ plane, (target % INNER) ^ inner
        if n < span:
            position_ref[n : n + 1, :] = (place_in * planes + group) * room + within
        here = (group_at == group) & (place_in == 0)
        high = jnp.where(here, (slot >> 4).astype(jnp.float32), 0.0)
        low = jnp.where(here, (slot & 15).astype(jnp.float32), 0.0)
        both = jnp.concatenate([high, low], axis=0).astype(jnp.bfloat16)
        filled = (room_at == within).astype(jnp.float32).astype(jnp.bfloat16)
        found = lax.dot_general(both, filled, (((1,), (1,)), ((), ())), preferred_element_type=jnp.float32)
        half = group_at.shape[0]
        value = found[:half] * 16.0 + found[half:] - 1.0
        slots_ref[n] = value[:planes].astype(jnp.int32)


def route(own, known, shift, planes, span, room):
    sources, tok_count = known.shape
    position, slots = pl.pallas_call(
        functools.partial(route_kernel, shift),
        in_specs=[pl.BlockSpec(memory_space=pltpu.SMEM), pl.BlockSpec((sources, tok_count), lambda: (0, 0))],
        out_shape=[
            jax.ShapeDtypeStruct((span, tok_count), jnp.int32),
            jax.ShapeDtypeStruct((sources, planes, room), jnp.int32),
        ],
        compiler_params=PARAMS,
        cost_estimate=COST,
    )(own, known)
    return position, jnp.transpose(slots, (1, 0, 2)).reshape(planes, 1, sources * room)


def pack_kernel(sources, position_ref, scale_ref, *refs):
    rows_refs, out_refs = refs[:sources], refs[sources:]
    count = out_refs[0].shape[1]
    for r, rows_ref in enumerate(rows_refs):
        rows = rows_ref[...]
        for k, out_ref in enumerate(out_refs):
            places = lax.broadcasted_iota(jnp.int32, (count, rows.shape[0]), 0) + k * count
            chosen = (places == position_ref[r : r + 1, :]).astype(jnp.float32)
            scale = jnp.sum(chosen * scale_ref[r : r + 1, :], axis=1, keepdims=True)
            picked = jnp.dot(chosen.astype(jnp.bfloat16), rows, preferred_element_type=jnp.float32)
            out_ref[r] = (picked * scale).astype(jnp.bfloat16)


def pack(position, scale, rows, count):
    sources, width = len(rows), rows[0].shape[1]
    return pl.pallas_call(
        functools.partial(pack_kernel, sources),
        out_shape=[jax.ShapeDtypeStruct((sources, count, width), jnp.bfloat16)] * INNER,
        compiler_params=PARAMS,
        cost_estimate=COST,
    )(position, scale, *rows)


def place_kernel(slots_ref, *refs):
    out_ref = refs[-1]
    rows = jnp.concatenate([ref[r, 0] for ref in refs[:-1] for r in range(ref.shape[0])], axis=0)
    tokens = lax.broadcasted_iota(jnp.int32, (out_ref.shape[1], rows.shape[0]), 0)
    chosen = (tokens == slots_ref[0]).astype(jnp.float32).astype(jnp.bfloat16)
    out_ref[0] = jnp.dot(chosen, rows, preferred_element_type=jnp.float32).astype(jnp.bfloat16)


def place(slots, pieces, tok_count):
    sources, groups, room, width = pieces[0].shape
    total = slots.shape[2]
    return pl.pallas_call(
        place_kernel,
        grid=(groups,),
        in_specs=[pl.BlockSpec((1, 1, total), lambda t: (t, 0, 0))]
        + [pl.BlockSpec((sources, 1, room, width), lambda t: (0, t, 0, 0))] * len(pieces),
        out_specs=pl.BlockSpec((1, tok_count, width), lambda t: (t, 0, 0)),
        out_shape=jax.ShapeDtypeStruct((groups, tok_count, width), jnp.bfloat16),
        compiler_params=PARAMS,
        cost_estimate=COST,
    )(slots, *pieces)


def product_kernel(n_rows, n_pieces, own_ref, *refs):
    leave_ref, keep_ref, weight_ref = refs[-3:]
    m, half = pl.program_id(0), pl.num_programs(0) // 2

    @pl.when(m == 0)
    def _():
        for k, ref in enumerate(refs[n_rows : n_rows + n_pieces]):
            depth = ref.shape[0]
            if n_pieces == 1:
                weight_ref[...] = ref[...]
            else:
                at = pl.multiple_of((k ^ own_ref[1]) * depth, 16)
                weight_ref[pl.ds(at, depth), :] = ref[...]

    total, start = None, 0
    for ref in refs[:n_rows]:
        stop = start + ref.shape[2]
        term = jnp.dot(ref[0], weight_ref[start:stop, :], preferred_element_type=jnp.float32)
        total = term if total is None else total + term
        start = stop

    @pl.when(m < half)
    def _():
        leave_ref[0] = total.astype(jnp.bfloat16)

    @pl.when(m >= half)
    def _():
        keep_ref[0] = total


def product(own, rows, pieces, block, columns):
    groups, tok_count = rows[0].shape[:2]
    width, half = sum(part.shape[2] for part in rows), groups // 2
    depth = pieces[0].shape[0]
    if depth % 16:
        places = jnp.arange(len(pieces), dtype=jnp.int32) ^ own[1]
        pieces = [jnp.stack(pieces)[places].reshape(width, -1)]
        depth = width
    in_specs = [pl.BlockSpec(memory_space=pltpu.SMEM)]
    in_specs += [
        pl.BlockSpec((1, tok_count, part.shape[2]), lambda m: (jnp.where(m < half, 2 * m + 1, 2 * (m - half)), 0, 0))
        for part in rows
    ]
    in_specs += [pl.BlockSpec((depth, columns), lambda m: (0, block))] * len(pieces)
    out_block = (1, tok_count, columns)
    return pl.pallas_call(
        functools.partial(product_kernel, len(rows), len(pieces)),
        grid=(groups,),
        in_specs=in_specs,
        out_specs=[
            pl.BlockSpec(out_block, lambda m: (jnp.minimum(m, half - 1), 0, 0)),
            pl.BlockSpec(out_block, lambda m: (jnp.maximum(m - half, 0), 0, 0)),
        ],
        out_shape=[
            jax.ShapeDtypeStruct((half, tok_count, columns), jnp.bfloat16),
            jax.ShapeDtypeStruct((half, tok_count, columns), jnp.float32),
        ],
        scratch_shapes=[pltpu.VMEM((width, columns), jnp.bfloat16)],
        compiler_params=PARAMS,
        cost_estimate=COST,
    )(own, *rows, *pieces)


def attend_kernel(heads, n_parts, *refs):
    parts = refs[:n_parts]
    doc_ref, doc_column_ref, q_ref, k_ref, v_ref = refs[n_parts : n_parts + 5]
    dq_ref, dk_ref, dv_ref = refs[-3:]
    count = q_ref.shape[0]
    factor = 1.0 / math.sqrt(HS)
    across = (((1,), (1,)), ((), ()))
    down = (((0,), (0,)), ((), ()))
    key_at = lax.broadcasted_iota(jnp.int32, (count, count), 0)
    query_at = lax.broadcasted_iota(jnp.int32, (count, count), 1)
    allowed = (doc_column_ref[...] == doc_ref[...]) & (key_at <= query_at)
    for h in range(heads):
        at = slice(h * HS, (h + 1) * HS)
        total = parts[0][0, :, at]
        for ref in parts[1:]:
            total = total + ref[0, :, at].astype(jnp.float32)
        grad = total.astype(jnp.bfloat16)
        q, k, v = q_ref[:, at], k_ref[:, at], v_ref[:, at]
        scores = lax.dot_general(k, q, across, preferred_element_type=jnp.float32) * factor
        scores = jnp.where(allowed, scores, -1e30)
        raised = jnp.exp(scores - jnp.max(scores, axis=0, keepdims=True))
        probs = raised * (1.0 / jnp.sum(raised, axis=0, keepdims=True))
        grad_p = lax.dot_general(v, grad, across, preferred_element_type=jnp.float32)
        delta = jnp.sum(probs * grad_p, axis=0, keepdims=True)
        grad_s = (probs * (grad_p - delta)).astype(jnp.bfloat16)
        probs_low = probs.astype(jnp.bfloat16)
        dv_ref[:, at] = jnp.dot(probs_low, grad, preferred_element_type=jnp.float32).astype(jnp.bfloat16)
        dk = jnp.dot(grad_s, q, preferred_element_type=jnp.float32) * factor
        dk_ref[:, at] = dk.astype(jnp.bfloat16)
        dq = lax.dot_general(grad_s, k, down, preferred_element_type=jnp.float32) * factor
        dq_ref[:, at] = dq.astype(jnp.bfloat16)


def attend(parts, first_head, heads, doc, query, key, value, old):
    tok_count, features = query.shape
    columns = heads * HS
    block = first_head // heads
    chunk_spec = pl.BlockSpec((tok_count, columns), lambda i: (0, block))
    in_specs = [pl.BlockSpec((1, tok_count, columns), lambda i: (0, 0, 0))] * len(parts)
    in_specs += [
        pl.BlockSpec((1, tok_count), lambda i: (0, 0)),
        pl.BlockSpec((tok_count, 1), lambda i: (0, 0)),
        chunk_spec,
        chunk_spec,
        chunk_spec,
    ]
    in_specs += [pl.BlockSpec(memory_space=pl.ANY)] * len(old)
    base = len(parts) + 5
    return pl.pallas_call(
        functools.partial(attend_kernel, heads, len(parts)),
        grid=(1,),
        in_specs=in_specs,
        out_specs=[chunk_spec] * 3,
        out_shape=[jax.ShapeDtypeStruct((tok_count, features), jnp.bfloat16)] * 3,
        input_output_aliases={base + n: n for n in range(len(old))},
        compiler_params=PARAMS,
        cost_estimate=COST,
    )(*parts, doc, doc.reshape(tok_count, 1), query, key, value, *old)


def cut(total, parts):
    tiles = total // 128
    sizes = [tiles // parts * 128 + (128 if n < tiles % parts else 0) for n in range(parts)]
    sizes[-1] += total - sum(sizes)
    return sizes


def shards(
    grad_blocks,
    row_scale,
    dest_peer,
    dest_slot,
    doc_ids,
    query_rows,
    key_rows,
    value_rows,
    out_weight,
):
    tok_count, width_part = grad_blocks.shape
    peers, cores = lax.axis_size("peer"), lax.axis_size("tp")
    planes = peers // INNER
    span = planes // cores
    width = width_part // span
    capacity = 2 * tok_count // peers
    room = -(-capacity // 16) * 16
    levels = planes.bit_length() - 1
    me, core = lax.axis_index("peer"), lax.axis_index("tp")
    plane, inner = me // INNER, me % INNER
    own = jnp.stack([plane, inner]).astype(jnp.int32)
    send = functools.partial(swap, peers=peers, cores=cores)

    def to_plane(array, r):
        def move(p, c):
            o, i = p // INNER, p % INNER
            return (c * span + ((o % span) ^ r)) * INNER + i, o // span

        return send(array, move=move)

    shift = (tok_count - 1).bit_length()
    known = ((dest_peer[:, 0] << shift) + dest_slot).astype(jnp.float32)
    known = jnp.stack([known, row_scale])
    near = jnp.stack([to_plane(known, r) for r in range(span)])
    known, scale = near[:, 0], near[:, 1]
    for step in (1, 2):
        known = jnp.concatenate([known, send(known, move=lambda p, c: (p ^ step, c))], axis=0)
    position, slots = route(own, known, shift, planes, span, room)

    widths = cut(width, ROW_PARTS)
    plane_rows, start = [], 0
    for size in widths:
        parts = []
        for r in range(span):
            at = ((plane % span) ^ r) * width + start
            part = lax.dynamic_slice(grad_blocks, (0, at), (tok_count, size))
            if start:
                part = after(part, near)
            parts.append(to_plane(part, r))
        plane_rows.append(parts)
        start += size

    weight = out_weight.T
    n_heads = weight.shape[1] // HS
    sixth = n_heads // 6
    heads = [sixth] * 5 + ([sixth // 2] * 2 if sixth % 2 == 0 else [sixth])
    firsts = [sum(heads[:n]) for n in range(len(heads))]
    group_of = [0, 0, 1, 1] + [2] * (len(heads) - 4)
    group_first = [0, 2 * sixth, 4 * sixth, n_heads]

    def gather_weight(g, hold):
        part = weight[:, group_first[g] * HS : group_first[g + 1] * HS]
        if hold is not None:
            part = after(part, hold)
        members = [[n * INNER + k for k in range(INNER)] for n in range(planes)]
        return [lax.all_gather(part, "peer", axis=0, tiled=True, axis_index_groups=members)]

    weights = [gather_weight(0, None)]

    rows, last, before, packed = [], None, None, None
    for parts in plane_rows:
        if packed is not None:
            parts = [after(parts[0], packed[0], *([] if before is None else [before]))] + parts[1:]
        packed = pack(position, scale, parts, planes * room)
        pieces = [packed[0]] + [send(packed[k], move=lambda p, c: (p ^ k, c)) for k in range(1, INNER)]
        if last is not None:
            pieces[0] = after(pieces[0], last)
        summed = place(slots, [one.reshape(span, planes, room, one.shape[2]) for one in pieces], tok_count)
        before, last = last, summed
        step = 1
        while step < cores:
            other = send(summed, move=lambda p, c: (p, c ^ step))
            summed = (summed.astype(jnp.float32) + other.astype(jnp.float32)).astype(jnp.bfloat16)
            step *= 2
        rows.append(summed)

    weights.append(gather_weight(1, last))
    weights.append(gather_weight(2, last))

    count = len(heads)
    last = rows[-1]
    leaving, arrived, kept = {}, {}, {}
    old = []

    def multiply(n):
        nonlocal last
        g = group_of[n]
        pieces = weights[g]
        first = (firsts[n] - group_first[g]) // heads[n]
        leaving[n], kept[n] = product(own, rows, [after(pieces[0], last)] + pieces[1:], first, heads[n] * HS)
        last = leaving[n]

    def launch(n, level, part):
        arrived.setdefault(n, []).append(send(part, move=lambda p, c: (p ^ (INNER << level), c)))

    def pass_on(n, level, *hold):
        nonlocal last
        part = after(kept[n], last, *hold)[1 << (level - 1) :: 1 << level]
        for j, one in enumerate(arrived[n]):
            part = part + one[1 << (level - j - 1) :: 1 << (level - j)].astype(jnp.float32)
        last = part.astype(jnp.bfloat16)
        launch(n, level, last)

    def finish(n):
        nonlocal old, last
        parts = [after(kept[n], last)] + arrived[n]
        old = attend(parts, firsts[n], heads[n], doc_ids, query_rows, key_rows, value_rows, old)
        last = old[0]

    for n in range(2):
        multiply(n)
        launch(n, 0, leaving[n])
    for n in range(count):
        for level in range(1, levels):
            pass_on(n, level, *(arrived[n - 1][-1:] if n else []))
        if n + 2 < count:
            multiply(n + 2)
            launch(n + 2, 0, leaving[n + 2])
        if n >= 1:
            finish(n - 1)
    finish(count - 1)
    return tuple(old)


def solution(mesh):
    return jax.shard_map(
        shards,
        mesh=mesh,
        in_specs=(
            P("peer", "tp"),
            P("peer"),
            P("peer", None),
            P("peer"),
            P("peer", None),
            P("peer", "tp"),
            P("peer", "tp"),
            P("peer", "tp"),
            P("tp", "peer"),
        ),
        out_specs=(P("peer", "tp"), P("peer", "tp"), P("peer", "tp")),
        check_vma=False,
    )
```

```python
import functools
import math

import jax
import jax.numpy as jnp
from jax import lax
from jax.experimental import pallas as pl
from jax.experimental.pallas import tpu as pltpu
from jax.sharding import PartitionSpec as P

HS = 128
INNER = 4
AXES = ("peer", "tp")
ROW_PARTS = 3
COST = pl.CostEstimate(flops=1000, bytes_accessed=1000, transcendentals=0)
PARAMS = pltpu.CompilerParams(vmem_limit_bytes=56 * 1024 * 1024)


def swap(array, peers, cores, move):
    pairs = []
    for peer in range(peers):
        for core in range(cores):
            to_peer, to_core = move(peer, core)
            pairs.append((peer * cores + core, to_peer * cores + to_core))
    return lax.ppermute(array, AXES, pairs)


def after(array, *others):
    return lax.optimization_barrier((array,) + others)[0]


def route_kernel(shift, own_ref, known_ref, position_ref, slots_ref):
    plane, inner, peers = own_ref[0], own_ref[1], slots_ref.shape[1] * INNER
    tok_count = known_ref.shape[1]
    sources, planes, room = slots_ref.shape
    span = position_ref.shape[0]
    rows = [known_ref[n : n + 1, :].astype(jnp.int32) for n in range(sources)]
    peer_at = lax.broadcasted_iota(jnp.int32, (peers, tok_count), 0)
    named = [(peer_at == (row >> shift)).astype(jnp.float32) for row in rows]
    before = (
        lax.broadcasted_iota(jnp.int32, (tok_count, tok_count), 0)
        < lax.broadcasted_iota(jnp.int32, (tok_count, tok_count), 1)
    ).astype(jnp.float32)
    counts = jnp.dot(
        jnp.concatenate(named, axis=0).astype(jnp.bfloat16),
        before.astype(jnp.bfloat16),
        preferred_element_type=jnp.float32,
    )
    group_at = lax.broadcasted_iota(jnp.int32, (max(planes, 8), tok_count), 0)
    room_at = lax.broadcasted_iota(jnp.int32, (room, tok_count), 0)
    for n, row in enumerate(rows):
        target, slot = row >> shift, (row & ((1 << shift) - 1)) + 1
        within = jnp.sum(named[n] * counts[n * peers : (n + 1) * peers], axis=0, keepdims=True).astype(jnp.int32)
        group, place_in = (target // INNER) ^ plane, (target % INNER) ^ inner
        if n < span:
            position_ref[n : n + 1, :] = (place_in * planes + group) * room + within
        here = (group_at == group) & (place_in == 0)
        high = jnp.where(here, (slot >> 4).astype(jnp.float32), 0.0)
        low = jnp.where(here, (slot & 15).astype(jnp.float32), 0.0)
        both = jnp.concatenate([high, low], axis=0).astype(jnp.bfloat16)
        filled = (room_at == within).astype(jnp.float32).astype(jnp.bfloat16)
        found = lax.dot_general(both, filled, (((1,), (1,)), ((), ())), preferred_element_type=jnp.float32)
        half = group_at.shape[0]
        value = found[:half] * 16.0 + found[half:] - 1.0
        slots_ref[n] = value[:planes].astype(jnp.int32)


def route(own, known, shift, planes, span, room):
    sources, tok_count = known.shape
    position, slots = pl.pallas_call(
        functools.partial(route_kernel, shift),
        in_specs=[pl.BlockSpec(memory_space=pltpu.SMEM), pl.BlockSpec((sources, tok_count), lambda: (0, 0))],
        out_shape=[
            jax.ShapeDtypeStruct((span, tok_count), jnp.int32),
            jax.ShapeDtypeStruct((sources, planes, room), jnp.int32),
        ],
        compiler_params=PARAMS,
        cost_estimate=COST,
    )(own, known)
    return position, jnp.transpose(slots, (1, 0, 2)).reshape(planes, 1, sources * room)


def pack_kernel(sources, position_ref, scale_ref, *refs):
    rows_refs, out_refs = refs[:sources], refs[sources:]
    count = out_refs[0].shape[1]
    for r, rows_ref in enumerate(rows_refs):
        rows = rows_ref[...]
        for k, out_ref in enumerate(out_refs):
            places = lax.broadcasted_iota(jnp.int32, (count, rows.shape[0]), 0) + k * count
            chosen = (places == position_ref[r : r + 1, :]).astype(jnp.float32)
            scale = jnp.sum(chosen * scale_ref[r : r + 1, :], axis=1, keepdims=True)
            picked = jnp.dot(chosen.astype(jnp.bfloat16), rows, preferred_element_type=jnp.float32)
            out_ref[r] = (picked * scale).astype(jnp.bfloat16)


def pack(position, scale, rows, count):
    sources, width = len(rows), rows[0].shape[1]
    return pl.pallas_call(
        functools.partial(pack_kernel, sources),
        out_shape=[jax.ShapeDtypeStruct((sources, count, width), jnp.bfloat16)] * INNER,
        compiler_params=PARAMS,
        cost_estimate=COST,
    )(position, scale, *rows)


def place_kernel(slots_ref, *refs):
    out_ref = refs[-1]
    rows = jnp.concatenate([ref[r, 0] for ref in refs[:-1] for r in range(ref.shape[0])], axis=0)
    tokens = lax.broadcasted_iota(jnp.int32, (out_ref.shape[1], rows.shape[0]), 0)
    chosen = (tokens == slots_ref[0]).astype(jnp.float32).astype(jnp.bfloat16)
    out_ref[0] = jnp.dot(chosen, rows, preferred_element_type=jnp.float32).astype(jnp.bfloat16)


def place(slots, pieces, tok_count):
    sources, groups, room, width = pieces[0].shape
    total = slots.shape[2]
    return pl.pallas_call(
        place_kernel,
        grid=(groups,),
        in_specs=[pl.BlockSpec((1, 1, total), lambda t: (t, 0, 0))]
        + [pl.BlockSpec((sources, 1, room, width), lambda t: (0, t, 0, 0))] * len(pieces),
        out_specs=pl.BlockSpec((1, tok_count, width), lambda t: (t, 0, 0)),
        out_shape=jax.ShapeDtypeStruct((groups, tok_count, width), jnp.bfloat16),
        compiler_params=PARAMS,
        cost_estimate=COST,
    )(slots, *pieces)


def product_kernel(n_rows, n_pieces, own_ref, *refs):
    leave_ref, keep_ref, weight_ref = refs[-3:]
    m, half = pl.program_id(0), pl.num_programs(0) // 2

    @pl.when(m == 0)
    def _():
        for k, ref in enumerate(refs[n_rows : n_rows + n_pieces]):
            depth = ref.shape[0]
            if n_pieces == 1:
                weight_ref[...] = ref[...]
            else:
                at = pl.multiple_of((k ^ own_ref[1]) * depth, 16)
                weight_ref[pl.ds(at, depth), :] = ref[...]

    total, start = None, 0
    for ref in refs[:n_rows]:
        stop = start + ref.shape[2]
        term = jnp.dot(ref[0], weight_ref[start:stop, :], preferred_element_type=jnp.float32)
        total = term if total is None else total + term
        start = stop

    @pl.when(m < half)
    def _():
        leave_ref[0] = total.astype(jnp.bfloat16)

    @pl.when(m >= half)
    def _():
        keep_ref[0] = total


def product(own, rows, pieces, block, columns):
    groups, tok_count = rows[0].shape[:2]
    width, half = sum(part.shape[2] for part in rows), groups // 2
    depth = pieces[0].shape[0]
    if depth % 16:
        places = jnp.arange(len(pieces), dtype=jnp.int32) ^ own[1]
        pieces = [jnp.stack(pieces)[places].reshape(width, -1)]
        depth = width
    in_specs = [pl.BlockSpec(memory_space=pltpu.SMEM)]
    in_specs += [
        pl.BlockSpec((1, tok_count, part.shape[2]), lambda m: (jnp.where(m < half, 2 * m + 1, 2 * (m - half)), 0, 0))
        for part in rows
    ]
    in_specs += [pl.BlockSpec((depth, columns), lambda m: (0, block))] * len(pieces)
    out_block = (1, tok_count, columns)
    return pl.pallas_call(
        functools.partial(product_kernel, len(rows), len(pieces)),
        grid=(groups,),
        in_specs=in_specs,
        out_specs=[
            pl.BlockSpec(out_block, lambda m: (jnp.minimum(m, half - 1), 0, 0)),
            pl.BlockSpec(out_block, lambda m: (jnp.maximum(m - half, 0), 0, 0)),
        ],
        out_shape=[
            jax.ShapeDtypeStruct((half, tok_count, columns), jnp.bfloat16),
            jax.ShapeDtypeStruct((half, tok_count, columns), jnp.float32),
        ],
        scratch_shapes=[pltpu.VMEM((width, columns), jnp.bfloat16)],
        compiler_params=PARAMS,
        cost_estimate=COST,
    )(own, *rows, *pieces)


def attend_kernel(heads, n_parts, *refs):
    parts = refs[:n_parts]
    doc_ref, doc_column_ref, q_ref, k_ref, v_ref = refs[n_parts : n_parts + 5]
    dq_ref, dk_ref, dv_ref = refs[-3:]
    count = q_ref.shape[0]
    factor = 1.0 / math.sqrt(HS)
    across = (((1,), (1,)), ((), ()))
    down = (((0,), (0,)), ((), ()))
    key_at = lax.broadcasted_iota(jnp.int32, (count, count), 0)
    query_at = lax.broadcasted_iota(jnp.int32, (count, count), 1)
    allowed = (doc_column_ref[...] == doc_ref[...]) & (key_at <= query_at)
    for h in range(heads):
        at = slice(h * HS, (h + 1) * HS)
        total = parts[0][0, :, at]
        for ref in parts[1:]:
            total = total + ref[0, :, at].astype(jnp.float32)
        grad = total.astype(jnp.bfloat16)
        q, k, v = q_ref[:, at], k_ref[:, at], v_ref[:, at]
        scores = lax.dot_general(k, q, across, preferred_element_type=jnp.float32) * factor
        scores = jnp.where(allowed, scores, -1e30)
        raised = jnp.exp(scores - jnp.max(scores, axis=0, keepdims=True))
        probs = raised * (1.0 / jnp.sum(raised, axis=0, keepdims=True))
        grad_p = lax.dot_general(v, grad, across, preferred_element_type=jnp.float32)
        delta = jnp.sum(probs * grad_p, axis=0, keepdims=True)
        grad_s = (probs * (grad_p - delta)).astype(jnp.bfloat16)
        probs_low = probs.astype(jnp.bfloat16)
        dv_ref[:, at] = jnp.dot(probs_low, grad, preferred_element_type=jnp.float32).astype(jnp.bfloat16)
        dk = jnp.dot(grad_s, q, preferred_element_type=jnp.float32) * factor
        dk_ref[:, at] = dk.astype(jnp.bfloat16)
        dq = lax.dot_general(grad_s, k, down, preferred_element_type=jnp.float32) * factor
        dq_ref[:, at] = dq.astype(jnp.bfloat16)


def attend(parts, first_head, heads, doc, query, key, value, old):
    tok_count, features = query.shape
    columns = heads * HS
    block = first_head // heads
    chunk_spec = pl.BlockSpec((tok_count, columns), lambda i: (0, block))
    in_specs = [pl.BlockSpec((1, tok_count, columns), lambda i: (0, 0, 0))] * len(parts)
    in_specs += [
        pl.BlockSpec((1, tok_count), lambda i: (0, 0)),
        pl.BlockSpec((tok_count, 1), lambda i: (0, 0)),
        chunk_spec,
        chunk_spec,
        chunk_spec,
    ]
    in_specs += [pl.BlockSpec(memory_space=pl.ANY)] * len(old)
    base = len(parts) + 5
    return pl.pallas_call(
        functools.partial(attend_kernel, heads, len(parts)),
        grid=(1,),
        in_specs=in_specs,
        out_specs=[chunk_spec] * 3,
        out_shape=[jax.ShapeDtypeStruct((tok_count, features), jnp.bfloat16)] * 3,
        input_output_aliases={base + n: n for n in range(len(old))},
        compiler_params=PARAMS,
        cost_estimate=COST,
    )(*parts, doc, doc.reshape(tok_count, 1), query, key, value, *old)


def cut(total, parts):
    tiles = total // 128
    sizes = [tiles // parts * 128 + (128 if n < tiles % parts else 0) for n in range(parts)]
    sizes[-1] += total - sum(sizes)
    return sizes


def shards(
    grad_blocks,
    row_scale,
    dest_peer,
    dest_slot,
    doc_ids,
    query_rows,
    key_rows,
    value_rows,
    out_weight,
):
    tok_count, width_part = grad_blocks.shape
    peers, cores = lax.axis_size("peer"), lax.axis_size("tp")
    planes = peers // INNER
    span = planes // cores
    width = width_part // span
    capacity = 2 * tok_count // peers
    room = -(-capacity // 16) * 16
    levels = planes.bit_length() - 1
    me, core = lax.axis_index("peer"), lax.axis_index("tp")
    plane, inner = me // INNER, me % INNER
    own = jnp.stack([plane, inner]).astype(jnp.int32)
    send = functools.partial(swap, peers=peers, cores=cores)

    def to_plane(array, r):
        def move(p, c):
            o, i = p // INNER, p % INNER
            return (c * span + ((o % span) ^ r)) * INNER + i, o // span

        return send(array, move=move)

    shift = (tok_count - 1).bit_length()
    known = ((dest_peer[:, 0] << shift) + dest_slot).astype(jnp.float32)
    known = jnp.stack([known, row_scale])
    near = jnp.stack([to_plane(known, r) for r in range(span)])
    known, scale = near[:, 0], near[:, 1]
    for step in (1, 2):
        known = jnp.concatenate([known, send(known, move=lambda p, c: (p ^ step, c))], axis=0)
    position, slots = route(own, known, shift, planes, span, room)

    widths = cut(width, ROW_PARTS)
    plane_rows, start = [], 0
    for size in widths:
        parts = []
        for r in range(span):
            at = ((plane % span) ^ r) * width + start
            part = lax.dynamic_slice(grad_blocks, (0, at), (tok_count, size))
            if start:
                part = after(part, near)
            parts.append(to_plane(part, r))
        plane_rows.append(parts)
        start += size

    weight = out_weight.T
    n_heads = weight.shape[1] // HS
    sixth = n_heads // 6
    heads = [sixth] * 5 + ([sixth // 2] * 2 if sixth % 2 == 0 else [sixth])
    firsts = [sum(heads[:n]) for n in range(len(heads))]
    group_of = [0, 0, 1, 1] + [2] * (len(heads) - 4)
    group_first = [0, 2 * sixth, 4 * sixth, n_heads]

    def gather_weight(g, hold):
        part = weight[:, group_first[g] * HS : group_first[g + 1] * HS]
        if hold is not None:
            part = after(part, hold)
        members = [[n * INNER + k for k in range(INNER)] for n in range(planes)]
        return [lax.all_gather(part, "peer", axis=0, tiled=True, axis_index_groups=members)]

    weights = [gather_weight(0, None)]

    rows, last, before, packed = [], None, None, None
    for parts in plane_rows:
        if packed is not None:
            parts = [after(parts[0], packed[0], *([] if before is None else [before]))] + parts[1:]
        packed = pack(position, scale, parts, planes * room)
        pieces = [packed[0]] + [send(packed[k], move=lambda p, c: (p ^ k, c)) for k in range(1, INNER)]
        if last is not None:
            pieces[0] = after(pieces[0], last)
        summed = place(slots, [one.reshape(span, planes, room, one.shape[2]) for one in pieces], tok_count)
        before, last = last, summed
        step = 1
        while step < cores:
            other = send(summed, move=lambda p, c: (p, c ^ step))
            summed = (summed.astype(jnp.float32) + other.astype(jnp.float32)).astype(jnp.bfloat16)
            step *= 2
        rows.append(summed)

    weights.append(gather_weight(1, last))
    weights.append(gather_weight(2, last))

    count = len(heads)
    last = rows[-1]
    leaving, arrived, kept = {}, {}, {}
    old = []

    def multiply(n):
        nonlocal last
        g = group_of[n]
        pieces = weights[g]
        first = (firsts[n] - group_first[g]) // heads[n]
        leaving[n], kept[n] = product(own, rows, [after(pieces[0], last)] + pieces[1:], first, heads[n] * HS)
        last = leaving[n]

    def launch(n, level, part):
        arrived.setdefault(n, []).append(send(part, move=lambda p, c: (p ^ (INNER << level), c)))

    def pass_on(n, level, *hold):
        nonlocal last
        part = after(kept[n], last, *hold)[1 << (level - 1) :: 1 << level]
        for j, one in enumerate(arrived[n]):
            part = part + one[1 << (level - j - 1) :: 1 << (level - j)].astype(jnp.float32)
        last = part.astype(jnp.bfloat16)
        launch(n, level, last)

    def finish(n):
        nonlocal old, last
        parts = [after(kept[n], last)] + arrived[n]
        old = attend(parts, firsts[n], heads[n], doc_ids, query_rows, key_rows, value_rows, old)
        last = old[0]

    for n in range(2):
        multiply(n)
        launch(n, 0, leaving[n])
    for n in range(count):
        for level in range(1, levels):
            pass_on(n, level, *(arrived[n - 1][-1:] if 0 < n < count - 1 else []))
        if n + 2 < count:
            multiply(n + 2)
            launch(n + 2, 0, leaving[n + 2])
        if n >= 1:
            finish(n - 1)
    finish(count - 1)
    return tuple(old)


def solution(mesh):
    return jax.shard_map(
        shards,
        mesh=mesh,
        in_specs=(
            P("peer", "tp"),
            P("peer"),
            P("peer", None),
            P("peer"),
            P("peer", None),
            P("peer", "tp"),
            P("peer", "tp"),
            P("peer", "tp"),
            P("tp", "peer"),
        ),
        out_specs=(P("peer", "tp"), P("peer", "tp"), P("peer", "tp")),
        check_vma=False,
    )
```
